32 devices in a mesh: bricks: 8 (over z, x), groups: 4 (over y, core).
Axes of the slice: x: 2, y: 2, z: 4, core: 2. Of those that a mesh axis runs over, the one named last changes fastest.
Arguments:
- fields: bfloat16 [4, 48, 64, 512], P('groups', 'bricks'), may hold values from -6 to 6
- cotangent: bfloat16 [4, 48, 64, 512], P('groups', 'bricks'), may hold values from -6 to 6
- first_weight: bfloat16 [64, 1728], replicated, may hold values from -0.15625 to 0.15625
- second_weight: bfloat16 [64, 1728], replicated, may hold values from -0.15625 to 0.15625
- counts: int32 [4, 8], P('groups', 'bricks'), may hold values from 2 to 6, as said below
- adjacency: int32 [4, 48, 6], P('groups', 'bricks'), may hold values from -1 to 47, as said below
Outputs:
- grad_fields: bfloat16 [4, 48, 64, 512], P('groups', 'bricks')
- grad_first: float32 [64, 1728], replicated
- grad_second: float32 [64, 1728], replicated
The draws below stay inside these ranges and needn't reach their ends.
Inputs may be any that keep to these rules, and one draw needn't show every extreme that they name: `counts`: each group has some slab with 6 live bricks; live bricks fill the first slots of a slab. `adjacency`: entries point only to live slots and only from live slots; the relation is symmetric (slot t is the upper neighbour of s along k exactly when s is the lower neighbour of t); the lower neighbour along the first dimension lies in the same slab or the slab one index below, the upper one in the same slab or one index above; neighbours along the second and third dimensions lie in the same slab.
All inputs are finite; a program needn't handle non-finite values.
Results may differ from the reference program's by a relative error of at most 0.0049.
Values may be sent and summed in bfloat16 or wider, within the bound.
A program may use at most 128 MiB of HBM per device.

```python
import jax
import jax.numpy as jnp
from jax import lax

C = 64
S = 8
MAXB = 6
CELLS = 512
KC = 1728
BDEV = 8
SLOTS = 48
GROUPS = 4


def brick_layout(key):
    base_key = jax.random.fold_in(key, 29)
    key_count, key_full, key_place = jax.random.split(base_key, 3)
    counts = jax.random.randint(key_count, (GROUPS, BDEV), 2, MAXB + 1)
    full_dev = jax.random.randint(key_full, (GROUPS,), 0, BDEV)
    counts = jnp.where(jnp.arange(BDEV)[None, :] == full_dev[:, None], MAXB, counts).astype(jnp.int32)
    scores = jax.random.randint(key_place, (GROUPS, BDEV, 18), 0, 4096) * 18 + jnp.arange(18)[None, None, :]
    position = jnp.arange(18)[None, None, :]
    scores = jnp.where(position == 4, -2, scores)
    scores = jnp.where(position == 13, -1, scores)
    places = jnp.argsort(scores, axis=-1)[:, :, :MAXB].astype(jnp.int32)
    owners = jnp.arange(BDEV, dtype=jnp.int32)[None, :, None]
    coord_one = (2 * owners + places // 9).reshape(GROUPS, SLOTS)
    coord_two = (places // 3 % 3).reshape(GROUPS, SLOTS)
    coord_three = (places % 3).reshape(GROUPS, SLOTS)
    live_slot = (jnp.arange(MAXB)[None, None, :] < counts[:, :, None]).reshape(GROUPS, SLOTS)
    place_code = jnp.where(live_slot, (coord_one * 3 + coord_two) * 3 + coord_three, -1)
    columns = []
    for dimension in range(3):
        for step_sign in (-1, 1):
            moved_one = coord_one + (step_sign if dimension == 0 else 0)
            moved_two = coord_two + (step_sign if dimension == 1 else 0)
            moved_three = coord_three + (step_sign if dimension == 2 else 0)
            inside = (moved_one >= 0) & (moved_one < 2 * BDEV) & (moved_two >= 0) & (moved_two < 3) & (moved_three >= 0) & (moved_three < 3)
            target = jnp.where(inside, (moved_one * 3 + moved_two) * 3 + moved_three, -2)
            matches = (target[:, :, None] == place_code[:, None, :]).astype(jnp.int32)
            found = jnp.max(matches, axis=-1) > 0
            where_found = jnp.argmax(matches, axis=-1).astype(jnp.int32)
            columns.append(jnp.where(found & live_slot, where_found, -1))
    return (counts, jnp.stack(columns, -1).astype(jnp.int32))


def draw_counts(key, part):
    return brick_layout(key)[0]


def draw_adjacency(key, part):
    return brick_layout(key)[1]


def shard_levels(rng, shape, shards, smallest, top_value):
    def one(dim, blocks):
        steps = jax.random.uniform(jax.random.fold_in(jax.random.fold_in(rng, 6), dim), (blocks,), jnp.float32, smallest / len(shards), top_value / len(shards))
        return jnp.repeat(jnp.exp(steps), shape[dim] // blocks).reshape((-1,) + (1,) * (len(shape) - dim - 1))

    loudness = one(*shards[0])
    for cut in shards[1:]:
        loudness = loudness * one(*cut)
    return loudness


def gaussian(key, shape, width, limit, cuts=(), kind=jnp.bfloat16):
    entries = jax.random.normal(key, shape, jnp.float32) * width
    if len(cuts) > 0:
        entries = shard_levels(key, shape, cuts, -0.22, 0.18) * entries
    return jnp.clip(entries, min=-limit, max=limit).astype(kind)


def setup_inputs(seed: int = 0) -> dict:
    splits = jax.random.split(jax.random.key(seed), 7)
    fields = gaussian(splits[0], (GROUPS, SLOTS, C, CELLS), 1.0, 6.0, ((0, 4), (1, 8)))
    cotangent = gaussian(splits[1], (GROUPS, SLOTS, C, CELLS), 1.0, 6.0, ((0, 4), (1, 8)))
    first_weight = gaussian(splits[2], (C, KC), KC ** -0.5, 0.15625)
    second_weight = gaussian(splits[3], (C, KC), KC ** -0.5, 0.15625)
    counts = draw_counts(jax.random.fold_in(splits[6], 71), 0)
    adjacency = draw_adjacency(jax.random.fold_in(splits[6], 71), 0)
    return {"fields": fields, "cotangent": cotangent, "first_weight": first_weight, "second_weight": second_weight, "counts": counts, "adjacency": adjacency}


def forward_conv(padded, kernel):
    return lax.conv_general_dilated(padded, kernel, (1, 1, 1), 'VALID', dimension_numbers=('NCDHW', 'OIDHW', 'NCDHW'), preferred_element_type=jnp.float32)

def transposed_conv(grads, kernel):
    widened = jnp.pad(grads, ((0, 0), (0, 0), (2, 2), (2, 2), (2, 2)))
    return lax.conv_general_dilated(widened, jnp.flip(kernel, (2, 3, 4)), (1, 1, 1), 'VALID', dimension_numbers=('NCDHW', 'IODHW', 'NCDHW'), preferred_element_type=jnp.float32)

def kernel_grad(padded, grads):
    result = lax.conv_general_dilated(padded, grads, (1, 1, 1), 'VALID', dimension_numbers=('CNDHW', 'IODHW', 'NCDHW'), preferred_element_type=jnp.float32)
    return jnp.transpose(result, (1, 0, 2, 3, 4))

def fetch_rows(layers, source):
    is_valid = source >= 0
    taken = jnp.take(layers, jnp.clip(source, 0, layers.shape[0] - 1), axis=0)
    shape_mask = is_valid.reshape((-1,) + (1,) * (layers.ndim - 1))
    return jnp.where(shape_mask, taken, jnp.zeros_like(taken))

def extend(values, neighbours, dimension):
    layer_axis = dimension + 2
    extent = values.shape[layer_axis]
    low_layers = lax.index_in_dim(values, 0, layer_axis, keepdims=False)
    high_layers = lax.index_in_dim(values, extent - 1, layer_axis, keepdims=False)
    into_low = fetch_rows(high_layers, neighbours[:, 2 * dimension])
    into_high = fetch_rows(low_layers, neighbours[:, 2 * dimension + 1])
    return jnp.concatenate([jnp.expand_dims(into_low, layer_axis), values, jnp.expand_dims(into_high, layer_axis)], layer_axis)

def retract(grads, neighbours, dimension):
    layer_axis = dimension + 2
    extent = grads.shape[layer_axis]
    low_rims = lax.index_in_dim(grads, 0, layer_axis, keepdims=False)
    high_rims = lax.index_in_dim(grads, extent - 1, layer_axis, keepdims=False)
    interior = lax.slice_in_dim(grads, 1, extent - 1, axis=layer_axis)
    add_low = fetch_rows(high_rims, neighbours[:, 2 * dimension])
    add_high = fetch_rows(low_rims, neighbours[:, 2 * dimension + 1])
    front_layer = lax.slice_in_dim(interior, 0, 1, axis=layer_axis) + jnp.expand_dims(add_low, layer_axis)
    back_layer = lax.slice_in_dim(interior, extent - 3, extent - 2, axis=layer_axis) + jnp.expand_dims(add_high, layer_axis)
    middle = lax.slice_in_dim(interior, 1, extent - 3, axis=layer_axis)
    return jnp.concatenate([front_layer, middle, back_layer], layer_axis)

def reference(fields, cotangent, first_weight, second_weight, counts, adjacency):
    kernel_one = first_weight.reshape(C, C, 3, 3, 3)
    kernel_two = second_weight.reshape(C, C, 3, 3, 3)
    sum_first = jnp.zeros((C, C, 3, 3, 3), jnp.float32)
    sum_second = jnp.zeros((C, C, 3, 3, 3), jnp.float32)
    outputs = []
    slot_ids = jnp.arange(SLOTS, dtype=jnp.int32)
    for group_id in range(GROUPS):
        neighbours = adjacency[group_id]
        owner_count = jnp.repeat(counts[group_id], MAXB)
        keep_mask = (slot_ids % MAXB < owner_count).astype(jnp.bfloat16)[:, None, None, None, None]
        inputs = fields[group_id].reshape(SLOTS, C, S, S, S) * keep_mask
        grads = cotangent[group_id].reshape(SLOTS, C, S, S, S) * keep_mask
        padded_in = inputs
        for dimension in range(3):
            padded_in = extend(padded_in, neighbours, dimension)
        pre_act = forward_conv(padded_in, kernel_one)
        gate_sig = jax.nn.sigmoid(pre_act)
        hidden = (pre_act * gate_sig).astype(jnp.bfloat16)
        padded_hidden = hidden
        for dimension in range(3):
            padded_hidden = extend(padded_hidden, neighbours, dimension)
        sum_second = sum_second + kernel_grad(padded_hidden, grads)
        back_hidden = transposed_conv(grads, kernel_two)
        for dimension in (2, 1, 0):
            back_hidden = retract(back_hidden, neighbours, dimension)
        d_pre = (back_hidden * gate_sig * (1.0 + pre_act * (1.0 - gate_sig))).astype(jnp.bfloat16)
        sum_first = sum_first + kernel_grad(padded_in, d_pre)
        back_in = transposed_conv(d_pre, kernel_one)
        for dimension in (2, 1, 0):
            back_in = retract(back_in, neighbours, dimension)
        outputs.append(back_in.astype(jnp.bfloat16).reshape(SLOTS, C, CELLS))
    factor = 1.0 / jnp.sqrt(jnp.float32(GROUPS * SLOTS * CELLS))
    grad_first = (sum_first * factor).reshape(C, KC)
    grad_second = (sum_second * factor).reshape(C, KC)
    return (jnp.stack(outputs, 0), grad_first, grad_second)
```

```python
import functools

import jax
import jax.numpy as jnp
from jax import lax
from jax.experimental import pallas as pl
from jax.experimental.pallas import tpu as pltpu
from jax.sharding import PartitionSpec as P

S = 8
LANES = 128
BF = jnp.bfloat16
F32 = jnp.float32
MESH = pl.DeviceIdType.MESH


def chunk(j):
    return slice(j * LANES, (j + 1) * LANES)


def shifted(own, nbr, width, step, coord):
    if step > 0:
        return jnp.where(
            coord == 7, pltpu.roll(nbr, 7 * width, 1), pltpu.roll(own, LANES - width, 1)
        )
    return jnp.where(
        coord == 0, pltpu.roll(nbr, LANES - 7 * width, 1), pltpu.roll(own, width, 1)
    )


def level_kernel(
    count_ref, adj_ref, f_ref, c_ref, w1_ref, w2_ref, w3_ref,
    out_ref, g1_ref, g2_ref,
    base, fx, t_ref, x9, zc, zd, f3, h3, y_ref, gate, hidden, halo0, halo1, halo2, halo3,
    send_sem, recv_sem,
):
    slots, channels, cells = f_ref.shape
    count = cells // LANES
    b = lax.axis_index("bricks")
    last = lax.axis_size("bricks") - 1
    has_low, has_up = b > 0, b < last
    rows = 3 * channels
    halos = (halo0, halo1, halo2, halo3)
    barrier = pltpu.get_barrier_semaphore()

    @pl.when(has_low)
    def _():
        pl.semaphore_signal(barrier, inc=1, device_id={"bricks": b - 1}, device_id_type=MESH)

    @pl.when(has_up)
    def _():
        pl.semaphore_signal(barrier, inc=1, device_id={"bricks": b + 1}, device_id_type=MESH)

    def lanes(r):
        return lax.broadcasted_iota(jnp.int32, (r, LANES), 1)

    def local(s, k, step):
        n = adj_ref[s, 2 * k + (1 if step > 0 else 0)]
        return jnp.where(n < 0, slots, jnp.clip(n - b * slots, 0, slots))

    def across(s, step):
        n = adj_ref[s, 1 if step > 0 else 0]
        return jnp.where(n < 0, 3 * slots, jnp.clip(n - (b - 1) * slots, 0, 3 * slots))

    def copies(k):
        own = halos[k].at[pl.ds(slots, slots)]
        low = pltpu.make_async_remote_copy(
            src_ref=own, dst_ref=halos[k].at[pl.ds(2 * slots, slots)],
            send_sem=send_sem.at[k, 0], recv_sem=recv_sem.at[k, 0],
            device_id={"bricks": b - 1}, device_id_type=MESH,
        )
        up = pltpu.make_async_remote_copy(
            src_ref=own, dst_ref=halos[k].at[pl.ds(0, slots)],
            send_sem=send_sem.at[k, 1], recv_sem=recv_sem.at[k, 1],
            device_id={"bricks": b + 1}, device_id_type=MESH,
        )
        return low, up

    def send(k):
        low, up = copies(k)

        @pl.when(has_low)
        def _():
            low.start()

        @pl.when(has_up)
        def _():
            up.start()

    def arrive(k):
        low, up = copies(k)

        @pl.when(has_low)
        def _():
            low.wait_send()
            up.wait_recv()

        @pl.when(has_up)
        def _():
            up.wait_send()
            low.wait_recv()

    def each_slot(body):
        def step(s, carry):
            body(s)
            return carry

        lax.fori_loop(0, slots, step, 0)

    def stage(src, dst, s, k, parts, nrows):
        width = 8 if k == 1 else 1
        lane = lanes(nrows)
        coord = (lane // width) % 8
        low, up = local(s, k, -1), local(s, k, 1)
        for j in range(parts):
            own = src[s, :, chunk(j)]
            dst[0:nrows, chunk(j)] = shifted(own, src[low, :, chunk(j)], width, -1, coord)
            dst[nrows:2 * nrows, chunk(j)] = own
            dst[2 * nrows:3 * nrows, chunk(j)] = shifted(
                own, src[up, :, chunk(j)], width, 1, coord
            )

    def swap(a_low, a_high):
        return pltpu.roll(jnp.where(lanes(channels) < 64, a_low, a_high), 64, 1)

    def edges(first, final):
        return jnp.where(lanes(channels) < 64, first, final).astype(BF)

    def combine(s, k, j):
        zero, minus, plus = channels, 0, 2 * channels
        y_zero = y_ref[k, s, zero:zero + channels, chunk(j)]
        plus_here = y_ref[k, s, plus:plus + channels, chunk(j)]
        minus_here = y_ref[k, s, minus:minus + channels, chunk(j)]
        if j + 1 < count:
            plus_next = y_ref[k, s, plus:plus + channels, chunk(j + 1)]
        else:
            plus_next = halos[1 + 2 * k][across(s, 1)].astype(F32)
        if j > 0:
            minus_before = y_ref[k, s, minus:minus + channels, chunk(j - 1)]
        else:
            minus_before = halos[1 + 2 * k][across(s, -1)].astype(F32)
        return y_zero + swap(plus_next + minus_here, plus_here + minus_before)

    for k in range(4):
        halos[k][3 * slots] = jnp.zeros((channels, LANES), BF)

    @pl.when(jnp.logical_not(has_low))
    def _():
        for k in range(4):
            halos[k][pl.ds(0, slots)] = jnp.zeros((slots, channels, LANES), BF)

    @pl.when(jnp.logical_not(has_up))
    def _():
        for k in range(4):
            halos[k][pl.ds(2 * slots, slots)] = jnp.zeros((slots, channels, LANES), BF)

    base[slots] = jnp.zeros((channels, cells), BF)
    fx[slots] = jnp.zeros((channels, cells + LANES), BF)
    t_ref[slots] = jnp.zeros((rows, cells + LANES), BF)

    def mask_fields(s):
        keep = jnp.where(s < count_ref[0, 0], 1.0, 0.0).astype(F32)
        f = (f_ref[s].astype(F32) * keep).astype(BF)
        f3[s, channels:2 * channels, :] = f
        halos[0][slots + s] = edges(f[:, chunk(0)], f[:, chunk(count - 1)])
        base[s] = (c_ref[s].astype(F32) * keep).astype(BF)

    each_slot(mask_fields)

    pl.semaphore_wait(barrier, has_low.astype(jnp.int32) + has_up.astype(jnp.int32))
    send(0)

    def back_conv(k, w_ref, z_ref):
        each_slot(lambda s: stage(base, t_ref.at[s], s, 2, count, channels))

        def second(s):
            stage(t_ref, z_ref.at[s], s, 1, count, rows)
            y = jnp.dot(w_ref[...], z_ref[s], preferred_element_type=F32)
            y_ref[k, s] = y
            halos[1 + 2 * k][slots + s] = edges(
                y[2 * channels:, chunk(0)], y[:channels, chunk(count - 1)]
            )

        each_slot(second)
        send(1 + 2 * k)

    back_conv(0, w2_ref, zc)
    arrive(0)

    def widen(s):
        f = [f3[s, channels:2 * channels, chunk(j)] for j in range(count)]
        low, up = halos[0][across(s, -1)], halos[0][across(s, 1)]
        wide = [low] + f + [up]
        for j in range(count + 1):
            part = swap(wide[j + 1], wide[j])
            fx[s, :, chunk(j)] = part
            if j < count:
                f3[s, 0:channels, chunk(j)] = part
            if j > 0:
                f3[s, 2 * channels:3 * channels, chunk(j - 1)] = part

    each_slot(widen)
    each_slot(lambda s: stage(fx, t_ref.at[s], s, 1, count + 1, channels))

    def forward(s):
        stage(t_ref, x9, s, 2, count + 1, rows)
        y = jnp.dot(w1_ref[...], x9[...], preferred_element_type=F32)
        y_minus, y_zero, y_plus = y[:channels], y[channels:2 * channels], y[2 * channels:]
        h = []
        for j in range(count):
            pre = (
                y_minus[:, chunk(j)]
                + swap(y_zero[:, chunk(j + 1)], y_zero[:, chunk(j)])
                + y_plus[:, chunk(j + 1)]
            )
            sig = jax.nn.sigmoid(pre)
            gate[s, :, chunk(j)] = sig * (1.0 + pre * (1.0 - sig))
            h.append((pre * sig).astype(BF))
            hidden[s, :, chunk(j)] = h[-1]
        halos[2][slots + s] = edges(h[0], h[-1])

    each_slot(forward)
    send(2)
    arrive(1)

    def d_pre(s):
        for j in range(count):
            base[s, :, chunk(j)] = (combine(s, 0, j) * gate[s, :, chunk(j)]).astype(BF)

    each_slot(d_pre)
    back_conv(1, w3_ref, zd)
    arrive(2)

    def widen_hidden(s):
        h = [hidden[s, :, chunk(j)] for j in range(count)]
        wide = [halos[2][across(s, -1)]] + h + [halos[2][across(s, 1)]]
        for j in range(count + 1):
            part = swap(wide[j + 1], wide[j])
            if j < count:
                h3[s, 0:channels, chunk(j)] = part
                h3[s, channels:2 * channels, chunk(j)] = h[j]
            if j > 0:
                h3[s, 2 * channels:3 * channels, chunk(j - 1)] = part

    each_slot(widen_hidden)
    g1_ref[...] = jnp.zeros_like(g1_ref)
    g2_ref[...] = jnp.zeros_like(g2_ref)

    def weight_grads(s):
        nt = (((1,), (1,)), ((), ()))
        g2_ref[...] += lax.dot_general(zc[s], h3[s], nt, preferred_element_type=F32)
        g1_ref[...] += lax.dot_general(zd[s], f3[s], nt, preferred_element_type=F32)

    each_slot(weight_grads)
    arrive(3)

    def finish(s):
        for j in range(count):
            out_ref[s, :, chunk(j)] = combine(s, 1, j).astype(BF)

    each_slot(finish)


def on_device(fields, cotangent, first_weight, second_weight, counts, adjacency):
    slots, channels, cells = fields.shape[1:]
    w1 = first_weight.reshape(channels, channels, 3, 3, 3)
    w2 = second_weight.reshape(channels, channels, 3, 3, 3)
    rows, cols = 3 * channels, 9 * channels
    forward_w = jnp.transpose(w1, (2, 0, 4, 3, 1)).reshape(rows, cols)

    def backward_w(w):
        return jnp.transpose(jnp.flip(w, (2, 3, 4)), (2, 1, 3, 4, 0)).reshape(rows, cols)

    vmem = pl.BlockSpec(memory_space=pltpu.VMEM)
    smem = pl.BlockSpec(memory_space=pltpu.SMEM)
    grad_fields, g1, g2 = pl.pallas_call(
        level_kernel,
        out_shape=(
            jax.ShapeDtypeStruct((slots, channels, cells), BF),
            jax.ShapeDtypeStruct((cols, rows), F32),
            jax.ShapeDtypeStruct((cols, rows), F32),
        ),
        in_specs=[smem, smem] + [vmem] * 5,
        out_specs=(vmem, vmem, vmem),
        scratch_shapes=[
            pltpu.VMEM((slots + 1, channels, cells), BF),
            pltpu.VMEM((slots + 1, channels, cells + LANES), BF),
            pltpu.VMEM((slots + 1, rows, cells + LANES), BF),
            pltpu.VMEM((cols, cells + LANES), BF),
            pltpu.VMEM((slots, cols, cells), BF),
            pltpu.VMEM((slots, cols, cells), BF),
            pltpu.VMEM((slots, rows, cells), BF),
            pltpu.VMEM((slots, rows, cells), BF),
            pltpu.VMEM((2, slots, rows, cells), F32),
            pltpu.VMEM((slots, channels, cells), F32),
            pltpu.VMEM((slots, channels, cells), BF),
        ]
        + [pltpu.VMEM((3 * slots + 1, channels, LANES), BF)] * 4
        + [
            pltpu.SemaphoreType.DMA((4, 2)),
            pltpu.SemaphoreType.DMA((4, 2)),
        ],
        compiler_params=pltpu.CompilerParams(
            collective_id=0, has_side_effects=True, vmem_limit_bytes=50 * 1024 * 1024
        ),
    )(
        counts, adjacency[0], fields[0], cotangent[0],
        forward_w, backward_w(w2), backward_w(w1),
    )
    s1, s2 = lax.psum((g1, g2), ("bricks", "groups"))
    total = lax.axis_size("groups") * slots * lax.axis_size("bricks") * cells
    factor = 1.0 / jnp.sqrt(jnp.float32(total))

    def weight_out(g):
        g = jnp.flip(g.reshape(3, 3, channels, 3, channels), (0, 1)) * factor
        return jnp.transpose(g, (2, 4, 3, 0, 1)).reshape(channels, channels * 27)

    return (grad_fields[None], weight_out(s1), weight_out(s2))


def solution(mesh):
    return jax.shard_map(
        on_device,
        mesh=mesh,
        in_specs=(
            P("groups", "bricks", None, None),
            P("groups", "bricks", None, None),
            P(),
            P(),
            P("groups", "bricks"),
            P("groups", "bricks", None),
        ),
        out_specs=(P("groups", "bricks", None, None), P(), P()),
        check_vma=False,
    )
```

```python
import functools

import jax
import jax.numpy as jnp
from jax import lax
from jax.experimental import pallas as pl
from jax.experimental.pallas import tpu as pltpu
from jax.sharding import PartitionSpec as P

S = 8
LANES = 128
BF = jnp.bfloat16
F32 = jnp.float32
MESH = pl.DeviceIdType.MESH


def chunk(j):
    return slice(j * LANES, (j + 1) * LANES)


def shifted(own, nbr, width, step, coord):
    if step > 0:
        return jnp.where(
            coord == 7, pltpu.roll(nbr, 7 * width, 1), pltpu.roll(own, LANES - width, 1)
        )
    return jnp.where(
        coord == 0, pltpu.roll(nbr, LANES - 7 * width, 1), pltpu.roll(own, width, 1)
    )


def level_kernel(
    factor,
    count_ref, adj_ref, f_ref, c_ref, w1_ref, w2_ref, w3_ref,
    out_ref, g1_out, g2_out,
    base, fx, t_ref, x9, zc, zd, f3, h3, y_ref, gate, hidden, halo0, halo1, halo2, halo3,
    g1_ref, g2_ref, part, mid, total, from_groups, from_bricks,
    send_sem, recv_sem, sum_send, sum_recv,
):
    slots, channels, cells = f_ref.shape
    count = cells // LANES
    b = lax.axis_index("bricks")
    last = lax.axis_size("bricks") - 1
    has_low, has_up = b > 0, b < last
    rows = 3 * channels
    halos = (halo0, halo1, halo2, halo3)
    barrier = pltpu.get_barrier_semaphore()

    g = lax.axis_index("groups")
    brick_count, group_count = lax.axis_size("bricks"), lax.axis_size("groups")

    def greet(axis, me, size):
        def one(k, carry):
            pl.semaphore_signal(
                barrier, inc=1, device_id={axis: lax.rem(me + k, size)}, device_id_type=MESH
            )
            return carry

        lax.fori_loop(1, size, one, 0)

    greet("bricks", b, brick_count)
    greet("groups", g, group_count)

    def exchange(phase, axis, me, size, src, dst):
        def copy(k):
            peer = lax.rem(me + k, size)
            return pltpu.make_async_remote_copy(
                src_ref=src(peer), dst_ref=dst(k),
                send_sem=sum_send.at[phase, k], recv_sem=sum_recv.at[phase, k],
                device_id={axis: peer}, device_id_type=MESH,
            )

        def start(k, carry):
            copy(k).start()
            return carry

        def wait(k, carry):
            copy(k).wait()
            return carry

        lax.fori_loop(1, size, start, 0)
        return lambda: lax.fori_loop(1, size, wait, 0)

    def lanes(r):
        return lax.broadcasted_iota(jnp.int32, (r, LANES), 1)

    def local(s, k, step):
        n = adj_ref[s, 2 * k + (1 if step > 0 else 0)]
        return jnp.where(n < 0, slots, jnp.clip(n - b * slots, 0, slots))

    def across(s, step):
        n = adj_ref[s, 1 if step > 0 else 0]
        return jnp.where(n < 0, 3 * slots, jnp.clip(n - (b - 1) * slots, 0, 3 * slots))

    def copies(k):
        own = halos[k].at[pl.ds(slots, slots)]
        low = pltpu.make_async_remote_copy(
            src_ref=own, dst_ref=halos[k].at[pl.ds(2 * slots, slots)],
            send_sem=send_sem.at[k, 0], recv_sem=recv_sem.at[k, 0],
            device_id={"bricks": b - 1}, device_id_type=MESH,
        )
        up = pltpu.make_async_remote_copy(
            src_ref=own, dst_ref=halos[k].at[pl.ds(0, slots)],
            send_sem=send_sem.at[k, 1], recv_sem=recv_sem.at[k, 1],
            device_id={"bricks": b + 1}, device_id_type=MESH,
        )
        return low, up

    def send(k):
        low, up = copies(k)

        @pl.when(has_low)
        def _():
            low.start()

        @pl.when(has_up)
        def _():
            up.start()

    def arrive(k):
        low, up = copies(k)

        @pl.when(has_low)
        def _():
            low.wait_send()
            up.wait_recv()

        @pl.when(has_up)
        def _():
            up.wait_send()
            low.wait_recv()

    def each_slot(body):
        def step(s, carry):
            body(s)
            return carry

        lax.fori_loop(0, slots, step, 0)

    def stage(src, dst, s, k, parts, nrows, sign=1):
        width = 8 if k == 1 else 1
        lane = lanes(nrows)
        coord = (lane // width) % 8
        low, up = local(s, k, -1), local(s, k, 1)
        first, final = (0, 2 * nrows) if sign > 0 else (2 * nrows, 0)
        for j in range(parts):
            own = src[s, :, chunk(j)]
            dst[first:first + nrows, chunk(j)] = shifted(own, src[low, :, chunk(j)], width, -1, coord)
            dst[nrows:2 * nrows, chunk(j)] = own
            dst[final:final + nrows, chunk(j)] = shifted(
                own, src[up, :, chunk(j)], width, 1, coord
            )

    def swap(a_low, a_high):
        return pltpu.roll(jnp.where(lanes(channels) < 64, a_low, a_high), 64, 1)

    def edges(first, final):
        return jnp.where(lanes(channels) < 64, first, final).astype(BF)

    def combine(s, k, j):
        zero, minus, plus = channels, 2 * channels, 0
        y_zero = y_ref[k, s, zero:zero + channels, chunk(j)]
        plus_here = y_ref[k, s, plus:plus + channels, chunk(j)]
        minus_here = y_ref[k, s, minus:minus + channels, chunk(j)]
        if j + 1 < count:
            plus_next = y_ref[k, s, plus:plus + channels, chunk(j + 1)]
        else:
            plus_next = halos[1 + 2 * k][across(s, 1)].astype(F32)
        if j > 0:
            minus_before = y_ref[k, s, minus:minus + channels, chunk(j - 1)]
        else:
            minus_before = halos[1 + 2 * k][across(s, -1)].astype(F32)
        return y_zero + swap(plus_next + minus_here, plus_here + minus_before)

    for k in range(4):
        halos[k][3 * slots] = jnp.zeros((channels, LANES), BF)

    @pl.when(jnp.logical_not(has_low))
    def _():
        for k in range(4):
            halos[k][pl.ds(0, slots)] = jnp.zeros((slots, channels, LANES), BF)

    @pl.when(jnp.logical_not(has_up))
    def _():
        for k in range(4):
            halos[k][pl.ds(2 * slots, slots)] = jnp.zeros((slots, channels, LANES), BF)

    base[slots] = jnp.zeros((channels, cells), BF)
    fx[slots] = jnp.zeros((channels, cells + LANES), BF)
    t_ref[slots] = jnp.zeros((rows, cells + LANES), BF)

    def mask_fields(s):
        keep = jnp.where(s < count_ref[0, 0], 1.0, 0.0).astype(F32)
        f = (f_ref[s].astype(F32) * keep).astype(BF)
        f3[s, channels:2 * channels, :] = f
        halos[0][slots + s] = edges(f[:, chunk(0)], f[:, chunk(count - 1)])
        base[s] = (c_ref[s].astype(F32) * keep).astype(BF)

    each_slot(mask_fields)

    pl.semaphore_wait(barrier, brick_count + group_count - 2)
    send(0)

    def back_conv(k, w_ref, z_ref):
        each_slot(lambda s: stage(base, t_ref.at[s], s, 2, count, channels, -1))

        def second(s):
            stage(t_ref, z_ref.at[s], s, 1, count, rows, -1)
            y = jnp.dot(w_ref[...], z_ref[s], preferred_element_type=F32)
            y_ref[k, s] = y
            halos[1 + 2 * k][slots + s] = edges(
                y[:channels, chunk(0)], y[2 * channels:, chunk(count - 1)]
            )

        each_slot(second)
        send(1 + 2 * k)

    back_conv(0, w2_ref, zc)
    arrive(0)

    def widen(s):
        f = [f3[s, channels:2 * channels, chunk(j)] for j in range(count)]
        low, up = halos[0][across(s, -1)], halos[0][across(s, 1)]
        wide = [low] + f + [up]
        for j in range(count + 1):
            part = swap(wide[j + 1], wide[j])
            fx[s, :, chunk(j)] = part
            if j < count:
                f3[s, 0:channels, chunk(j)] = part
            if j > 0:
                f3[s, 2 * channels:3 * channels, chunk(j - 1)] = part

    each_slot(widen)
    each_slot(lambda s: stage(fx, t_ref.at[s], s, 1, count + 1, channels))

    def forward(s):
        stage(t_ref, x9, s, 2, count + 1, rows)
        y = jnp.dot(w1_ref[...], x9[...], preferred_element_type=F32)
        y_minus, y_zero, y_plus = y[:channels], y[channels:2 * channels], y[2 * channels:]
        h = []
        for j in range(count):
            pre = (
                y_minus[:, chunk(j)]
                + swap(y_zero[:, chunk(j + 1)], y_zero[:, chunk(j)])
                + y_plus[:, chunk(j + 1)]
            )
            sig = jax.nn.sigmoid(pre)
            gate[s, :, chunk(j)] = sig * (1.0 + pre * (1.0 - sig))
            h.append((pre * sig).astype(BF))
            hidden[s, :, chunk(j)] = h[-1]
        halos[2][slots + s] = edges(h[0], h[-1])

    each_slot(forward)
    send(2)
    arrive(1)

    def d_pre(s):
        for j in range(count):
            base[s, :, chunk(j)] = (combine(s, 0, j) * gate[s, :, chunk(j)]).astype(BF)

    each_slot(d_pre)
    back_conv(1, w3_ref, zd)
    arrive(2)

    def widen_hidden(s):
        h = [hidden[s, :, chunk(j)] for j in range(count)]
        wide = [halos[2][across(s, -1)]] + h + [halos[2][across(s, 1)]]
        for j in range(count + 1):
            part = swap(wide[j + 1], wide[j])
            if j < count:
                h3[s, 0:channels, chunk(j)] = part
                h3[s, channels:2 * channels, chunk(j)] = h[j]
            if j > 0:
                h3[s, 2 * channels:3 * channels, chunk(j - 1)] = part

    each_slot(widen_hidden)
    g1_ref[...] = jnp.zeros_like(g1_ref)
    g2_ref[...] = jnp.zeros_like(g2_ref)

    def weight_grads(s):
        nt = (((1,), (1,)), ((), ()))
        g2_ref[:, 0:rows] += lax.dot_general(zc[s], h3[s], nt, preferred_element_type=F32)
        g1_ref[:, 0:rows] += lax.dot_general(zd[s], f3[s], nt, preferred_element_type=F32)

    each_slot(weight_grads)

    units, unit_rows = part.shape[:2]
    cols = g1_ref.shape[0]
    span = cols // unit_rows
    wide = lax.broadcasted_iota(jnp.int32, (cols, LANES), 1)

    def put(at, value):
        part[at * span:(at + 1) * span] = value.astype(BF).reshape(span, unit_rows, LANES)

    put(0, g2_ref[:, 0:LANES])
    put(1, g1_ref[:, 0:LANES])
    put(2, jnp.where(
        wide < 64, g2_ref[:, LANES:2 * LANES], pltpu.roll(g1_ref[:, LANES:2 * LANES], 64, 1)
    ))
    part[3 * span:] = jnp.zeros((units - 3 * span, unit_rows, LANES), BF)
    own_units = pl.ds(g * brick_count, brick_count)
    own_unit = g * brick_count + b
    done = exchange(
        0, "groups", g, group_count,
        lambda peer: part.at[pl.ds(peer * brick_count, brick_count)], lambda k: from_groups.at[k],
    )
    arrive(3)

    def finish(s):
        for j in range(count):
            out_ref[s, :, chunk(j)] = combine(s, 1, j).astype(BF)

    each_slot(finish)
    done()
    acc = part[own_units].astype(F32)
    for k in range(1, group_count):
        acc = acc + from_groups[k].astype(F32)
    mid[...] = acc.astype(BF)
    exchange(
        1, "bricks", b, brick_count, lambda peer: mid.at[peer], lambda k: from_bricks.at[k]
    )()
    acc = mid[b].astype(F32)
    for k in range(1, brick_count):
        acc = acc + from_bricks[k].astype(F32)
    total[own_unit] = (acc * factor).astype(BF)
    exchange(
        2, "bricks", b, brick_count,
        lambda peer: total.at[own_unit], lambda k: total.at[own_unit],
    )()
    exchange(
        3, "groups", g, group_count,
        lambda peer: total.at[own_units], lambda k: total.at[own_units],
    )()

    def get(at):
        return total[at * span:(at + 1) * span].reshape(cols, LANES).astype(F32)

    g2_out[:, 0:LANES] = get(0)
    g1_out[:, 0:LANES] = get(1)
    mixed = get(2)
    g2_out[:, LANES:rows] = mixed[:, 0:rows - LANES]
    g1_out[:, LANES:rows] = pltpu.roll(mixed, 64, 1)[:, 0:rows - LANES]


def on_device(fields, cotangent, first_weight, second_weight, counts, adjacency):
    slots, channels, cells = fields.shape[1:]
    w1 = first_weight.reshape(channels, channels, 3, 3, 3)
    w2 = second_weight.reshape(channels, channels, 3, 3, 3)
    rows, cols = 3 * channels, 9 * channels
    forward_w = jnp.transpose(w1, (2, 0, 4, 3, 1)).reshape(rows, cols)

    def backward_w(w):
        return jnp.transpose(w, (2, 1, 3, 4, 0)).reshape(rows, cols)

    brick_count, group_count = lax.axis_size("bricks"), lax.axis_size("groups")
    factor = float((group_count * slots * brick_count * cells) ** -0.5)
    devices = brick_count * group_count
    unit_rows = 16
    while devices * unit_rows * LANES < 2 * rows * cols or cols % unit_rows:
        unit_rows += 16
    unit = (unit_rows, LANES)
    peers = max(brick_count, group_count)
    vmem = pl.BlockSpec(memory_space=pltpu.VMEM)
    smem = pl.BlockSpec(memory_space=pltpu.SMEM)
    grad_fields, g1, g2 = pl.pallas_call(
        functools.partial(level_kernel, factor),
        out_shape=(
            jax.ShapeDtypeStruct((slots, channels, cells), BF),
            jax.ShapeDtypeStruct((cols, rows), F32),
            jax.ShapeDtypeStruct((cols, rows), F32),
        ),
        in_specs=[smem, smem] + [vmem] * 5,
        out_specs=(vmem, vmem, vmem),
        scratch_shapes=[
            pltpu.VMEM((slots + 1, channels, cells), BF),
            pltpu.VMEM((slots + 1, channels, cells + LANES), BF),
            pltpu.VMEM((slots + 1, rows, cells + LANES), BF),
            pltpu.VMEM((cols, cells + LANES), BF),
            pltpu.VMEM((slots, cols, cells), BF),
            pltpu.VMEM((slots, cols, cells), BF),
            pltpu.VMEM((slots, rows, cells), BF),
            pltpu.VMEM((slots, rows, cells), BF),
            pltpu.VMEM((2, slots, rows, cells), F32),
            pltpu.VMEM((slots, channels, cells), F32),
            pltpu.VMEM((slots, channels, cells), BF),
        ]
        + [pltpu.VMEM((3 * slots + 1, channels, LANES), BF)] * 4
        + [
            pltpu.VMEM((cols, 2 * LANES), F32),
            pltpu.VMEM((cols, 2 * LANES), F32),
            pltpu.VMEM((devices,) + unit, BF),
            pltpu.VMEM((brick_count,) + unit, BF),
            pltpu.VMEM((devices,) + unit, BF),
            pltpu.VMEM((group_count, brick_count) + unit, BF),
            pltpu.VMEM((brick_count,) + unit, BF),
            pltpu.SemaphoreType.DMA((4, 2)),
            pltpu.SemaphoreType.DMA((4, 2)),
            pltpu.SemaphoreType.DMA((4, peers)),
            pltpu.SemaphoreType.DMA((4, peers)),
        ],
        compiler_params=pltpu.CompilerParams(
            collective_id=0, has_side_effects=True, vmem_limit_bytes=50 * 1024 * 1024
        ),
    )(
        counts, adjacency[0], fields[0], cotangent[0],
        forward_w, backward_w(w2), backward_w(w1),
    )
    def weight_out(g):
        g = g.reshape(3, 3, channels, 3, channels)
        return jnp.transpose(g, (2, 4, 3, 0, 1)).reshape(channels, channels * 27)

    return (grad_fields[None], weight_out(g1), weight_out(g2))


def solution(mesh):
    return jax.shard_map(
        on_device,
        mesh=mesh,
        in_specs=(
            P("groups", "bricks", None, None),
            P("groups", "bricks", None, None),
            P(),
            P(),
            P("groups", "bricks"),
            P("groups", "bricks", None),
        ),
        out_specs=(P("groups", "bricks", None, None), P(), P()),
        check_vma=False,
    )
```

```python
import functools

import jax
import jax.numpy as jnp
from jax import lax
from jax.experimental import pallas as pl
from jax.experimental.pallas import tpu as pltpu
from jax.sharding import PartitionSpec as P

S = 8
LANES = 128
BF = jnp.bfloat16
F32 = jnp.float32
MESH = pl.DeviceIdType.MESH


def chunk(j):
    return slice(j * LANES, (j + 1) * LANES)


def shifted(own, nbr, width, step, coord):
    if step > 0:
        return jnp.where(
            coord == 7, pltpu.roll(nbr, 7 * width, 1), pltpu.roll(own, LANES - width, 1)
        )
    return jnp.where(
        coord == 0, pltpu.roll(nbr, LANES - 7 * width, 1), pltpu.roll(own, width, 1)
    )


def level_kernel(
    factor,
    count_ref, adj_ref, f_ref, c_ref, w1_ref, w2_ref, w3_ref,
    out_ref, g1_out, g2_out,
    base, fx, t_ref, x9, zc, zd, f3, h3, y_ref, gate, hidden, halo0, halo1, halo2, halo3,
    g1_ref, g2_ref, *rest,
):
    buffers = rest[:5], rest[5:10]
    send_sem, recv_sem, sum_send, sum_recv = rest[10:]
    slots, channels, cells = f_ref.shape
    count = cells // LANES
    b = lax.axis_index("bricks")
    last = lax.axis_size("bricks") - 1
    has_low, has_up = b > 0, b < last
    rows = 3 * channels
    halos = (halo0, halo1, halo2, halo3)
    barrier = pltpu.get_barrier_semaphore()

    g = lax.axis_index("groups")
    brick_count, group_count = lax.axis_size("bricks"), lax.axis_size("groups")

    def greet(axis, me, size):
        def one(k, carry):
            pl.semaphore_signal(
                barrier, inc=1, device_id={axis: lax.rem(me + k, size)}, device_id_type=MESH
            )
            return carry

        lax.fori_loop(1, size, one, 0)

    greet("bricks", b, brick_count)
    greet("groups", g, group_count)

    def exchange(phase, axis, me, size, src, dst):
        def copy(k):
            peer = lax.rem(me + k, size)
            return pltpu.make_async_remote_copy(
                src_ref=src(peer), dst_ref=dst(k),
                send_sem=sum_send.at[phase, k], recv_sem=sum_recv.at[phase, k],
                device_id={axis: peer}, device_id_type=MESH,
            )

        def start(k, carry):
            copy(k).start()
            return carry

        def wait(k, carry):
            copy(k).wait()
            return carry

        lax.fori_loop(1, size, start, 0)
        return lambda: lax.fori_loop(1, size, wait, 0)

    def lanes(r):
        return lax.broadcasted_iota(jnp.int32, (r, LANES), 1)

    def local(s, k, step):
        n = adj_ref[s, 2 * k + (1 if step > 0 else 0)]
        return jnp.where(n < 0, slots, jnp.clip(n - b * slots, 0, slots))

    def across(s, step):
        n = adj_ref[s, 1 if step > 0 else 0]
        return jnp.where(n < 0, 3 * slots, jnp.clip(n - (b - 1) * slots, 0, 3 * slots))

    def copies(k):
        own = halos[k].at[pl.ds(slots, slots)]
        low = pltpu.make_async_remote_copy(
            src_ref=own, dst_ref=halos[k].at[pl.ds(2 * slots, slots)],
            send_sem=send_sem.at[k, 0], recv_sem=recv_sem.at[k, 0],
            device_id={"bricks": b - 1}, device_id_type=MESH,
        )
        up = pltpu.make_async_remote_copy(
            src_ref=own, dst_ref=halos[k].at[pl.ds(0, slots)],
            send_sem=send_sem.at[k, 1], recv_sem=recv_sem.at[k, 1],
            device_id={"bricks": b + 1}, device_id_type=MESH,
        )
        return low, up

    def send(k):
        low, up = copies(k)

        @pl.when(has_low)
        def _():
            low.start()

        @pl.when(has_up)
        def _():
            up.start()

    def arrive(k):
        low, up = copies(k)

        @pl.when(has_low)
        def _():
            low.wait_send()
            up.wait_recv()

        @pl.when(has_up)
        def _():
            up.wait_send()
            low.wait_recv()

    def each_slot(body):
        def step(s, carry):
            body(s)
            return carry

        lax.fori_loop(0, slots, step, 0)

    def stage(src, dst, s, k, parts, nrows, sign=1):
        width = 8 if k == 1 else 1
        lane = lanes(nrows)
        coord = (lane // width) % 8
        low, up = local(s, k, -1), local(s, k, 1)
        first, final = (0, 2 * nrows) if sign > 0 else (2 * nrows, 0)
        for j in range(parts):
            own = src[s, :, chunk(j)]
            dst[first:first + nrows, chunk(j)] = shifted(own, src[low, :, chunk(j)], width, -1, coord)
            dst[nrows:2 * nrows, chunk(j)] = own
            dst[final:final + nrows, chunk(j)] = shifted(
                own, src[up, :, chunk(j)], width, 1, coord
            )

    def swap(a_low, a_high):
        return pltpu.roll(jnp.where(lanes(channels) < 64, a_low, a_high), 64, 1)

    def edges(first, final):
        return jnp.where(lanes(channels) < 64, first, final).astype(BF)

    def combine(s, k, j):
        zero, minus, plus = channels, 2 * channels, 0
        y_zero = y_ref[k, s, zero:zero + channels, chunk(j)]
        plus_here = y_ref[k, s, plus:plus + channels, chunk(j)]
        minus_here = y_ref[k, s, minus:minus + channels, chunk(j)]
        if j + 1 < count:
            plus_next = y_ref[k, s, plus:plus + channels, chunk(j + 1)]
        else:
            plus_next = halos[1 + 2 * k][across(s, 1)].astype(F32)
        if j > 0:
            minus_before = y_ref[k, s, minus:minus + channels, chunk(j - 1)]
        else:
            minus_before = halos[1 + 2 * k][across(s, -1)].astype(F32)
        return y_zero + swap(plus_next + minus_here, plus_here + minus_before)

    for k in range(4):
        halos[k][3 * slots] = jnp.zeros((channels, LANES), BF)

    @pl.when(jnp.logical_not(has_low))
    def _():
        for k in range(4):
            halos[k][pl.ds(0, slots)] = jnp.zeros((slots, channels, LANES), BF)

    @pl.when(jnp.logical_not(has_up))
    def _():
        for k in range(4):
            halos[k][pl.ds(2 * slots, slots)] = jnp.zeros((slots, channels, LANES), BF)

    base[slots] = jnp.zeros((channels, cells), BF)
    fx[slots] = jnp.zeros((channels, cells + LANES), BF)
    t_ref[slots] = jnp.zeros((rows, cells + LANES), BF)

    def mask_fields(s):
        keep = jnp.where(s < count_ref[0, 0], 1.0, 0.0).astype(F32)
        f = (f_ref[s].astype(F32) * keep).astype(BF)
        f3[s, channels:2 * channels, :] = f
        halos[0][slots + s] = edges(f[:, chunk(0)], f[:, chunk(count - 1)])
        base[s] = (c_ref[s].astype(F32) * keep).astype(BF)

    each_slot(mask_fields)

    pl.semaphore_wait(barrier, brick_count + group_count - 2)
    send(0)

    def back_conv(k, w_ref, z_ref):
        each_slot(lambda s: stage(base, t_ref.at[s], s, 2, count, channels, -1))

        def second(s):
            stage(t_ref, z_ref.at[s], s, 1, count, rows, -1)
            y = jnp.dot(w_ref[...], z_ref[s], preferred_element_type=F32)
            y_ref[k, s] = y
            halos[1 + 2 * k][slots + s] = edges(
                y[:channels, chunk(0)], y[2 * channels:, chunk(count - 1)]
            )

        each_slot(second)
        send(1 + 2 * k)

    back_conv(0, w2_ref, zc)
    arrive(0)

    def widen(s):
        f = [f3[s, channels:2 * channels, chunk(j)] for j in range(count)]
        low, up = halos[0][across(s, -1)], halos[0][across(s, 1)]
        wide = [low] + f + [up]
        for j in range(count + 1):
            part = swap(wide[j + 1], wide[j])
            fx[s, :, chunk(j)] = part
            if j < count:
                f3[s, 0:channels, chunk(j)] = part
            if j > 0:
                f3[s, 2 * channels:3 * channels, chunk(j - 1)] = part

    each_slot(widen)
    each_slot(lambda s: stage(fx, t_ref.at[s], s, 1, count + 1, channels))

    def forward(s):
        stage(t_ref, x9, s, 2, count + 1, rows)
        y = jnp.dot(w1_ref[...], x9[...], preferred_element_type=F32)
        y_minus, y_zero, y_plus = y[:channels], y[channels:2 * channels], y[2 * channels:]
        h = []
        for j in range(count):
            pre = (
                y_minus[:, chunk(j)]
                + swap(y_zero[:, chunk(j + 1)], y_zero[:, chunk(j)])
                + y_plus[:, chunk(j + 1)]
            )
            sig = jax.nn.sigmoid(pre)
            gate[s, :, chunk(j)] = sig * (1.0 + pre * (1.0 - sig))
            h.append((pre * sig).astype(BF))
            hidden[s, :, chunk(j)] = h[-1]
        halos[2][slots + s] = edges(h[0], h[-1])

    each_slot(forward)
    send(2)
    arrive(1)

    def d_pre(s):
        for j in range(count):
            base[s, :, chunk(j)] = (combine(s, 0, j) * gate[s, :, chunk(j)]).astype(BF)

    each_slot(d_pre)
    arrive(2)

    def widen_hidden(s):
        h = [hidden[s, :, chunk(j)] for j in range(count)]
        wide = [halos[2][across(s, -1)]] + h + [halos[2][across(s, 1)]]
        for j in range(count + 1):
            part = swap(wide[j + 1], wide[j])
            if j < count:
                h3[s, 0:channels, chunk(j)] = part
                h3[s, channels:2 * channels, chunk(j)] = h[j]
            if j > 0:
                h3[s, 2 * channels:3 * channels, chunk(j - 1)] = part

    each_slot(widen_hidden)
    own_units = pl.ds(g * brick_count, brick_count)
    own_unit = g * brick_count + b
    cols = g1_ref.shape[0]
    half = cols // 2
    low_lanes = lax.broadcasted_iota(jnp.int32, (half, LANES), 1) < 64

    def weight_grad(acc_ref, z_ref, source):
        acc_ref[...] = jnp.zeros_like(acc_ref)

        def add(s):
            acc_ref[:, 0:rows] += lax.dot_general(
                z_ref[s], source[s], (((1,), (1,)), ((), ())), preferred_element_type=F32
            )

        each_slot(add)

    def scatter_groups(i, acc_ref):
        part, from_groups = buffers[i][0], buffers[i][3]
        units, unit_rows = part.shape[:2]
        first, used = cols // unit_rows, 3 * half // unit_rows
        part[0:first] = acc_ref[:, 0:LANES].astype(BF).reshape(first, unit_rows, LANES)
        packed = jnp.where(
            low_lanes, acc_ref[0:half, LANES:2 * LANES],
            pltpu.roll(acc_ref[half:cols, LANES:2 * LANES], 64, 1),
        )
        part[first:used] = packed.astype(BF).reshape(used - first, unit_rows, LANES)
        part[used:] = jnp.zeros((units - used, unit_rows, LANES), BF)
        return exchange(
            4 * i, "groups", g, group_count,
            lambda peer: part.at[pl.ds(peer * brick_count, brick_count)],
            lambda k: from_groups.at[k],
        )

    def scatter_bricks(i):
        part, mid, _, from_groups, from_bricks = buffers[i]
        acc = part[own_units].astype(F32)
        for k in range(1, group_count):
            acc = acc + from_groups[k].astype(F32)
        mid[...] = acc.astype(BF)
        return exchange(
            4 * i + 1, "bricks", b, brick_count,
            lambda peer: mid.at[peer], lambda k: from_bricks.at[k],
        )

    def gather_bricks(i):
        _, mid, total, _, from_bricks = buffers[i]
        acc = mid[b].astype(F32)
        for k in range(1, brick_count):
            acc = acc + from_bricks[k].astype(F32)
        total[own_unit] = (acc * factor).astype(BF)
        return exchange(
            4 * i + 2, "bricks", b, brick_count,
            lambda peer: total.at[own_unit], lambda k: total.at[own_unit],
        )

    def gather_groups(i):
        total = buffers[i][2]
        return exchange(
            4 * i + 3, "groups", g, group_count,
            lambda peer: total.at[own_units], lambda k: total.at[own_units],
        )

    def unpack(i, out):
        total = buffers[i][2]
        unit_rows = total.shape[1]
        first, used = cols // unit_rows, 3 * half // unit_rows
        out[:, 0:LANES] = total[0:first].reshape(cols, LANES).astype(F32)
        packed = total[first:used].reshape(half, LANES).astype(F32)
        out[0:half, LANES:rows] = packed[:, 0:rows - LANES]
        out[half:cols, LANES:rows] = pltpu.roll(packed, 64, 1)[:, 0:rows - LANES]

    weight_grad(g2_ref, zc, h3)
    second_done = scatter_groups(0, g2_ref)
    back_conv(1, w3_ref, zd)
    second_done()
    second_done = scatter_bricks(0)
    weight_grad(g1_ref, zd, f3)
    first_done = scatter_groups(1, g1_ref)
    second_done()
    second_done = gather_bricks(0)
    arrive(3)

    def finish(s):
        for j in range(count):
            out_ref[s, :, chunk(j)] = combine(s, 1, j).astype(BF)

    each_slot(finish)
    first_done()
    first_done = scatter_bricks(1)
    second_done()
    second_done = gather_groups(0)
    first_done()
    first_done = gather_bricks(1)
    second_done()
    unpack(0, g2_out)
    first_done()
    gather_groups(1)()
    unpack(1, g1_out)


def on_device(fields, cotangent, first_weight, second_weight, counts, adjacency):
    slots, channels, cells = fields.shape[1:]
    w1 = first_weight.reshape(channels, channels, 3, 3, 3)
    w2 = second_weight.reshape(channels, channels, 3, 3, 3)
    rows, cols = 3 * channels, 9 * channels
    forward_w = jnp.transpose(w1, (2, 0, 4, 3, 1)).reshape(rows, cols)

    def backward_w(w):
        return jnp.transpose(w, (2, 1, 3, 4, 0)).reshape(rows, cols)

    brick_count, group_count = lax.axis_size("bricks"), lax.axis_size("groups")
    factor = float((group_count * slots * brick_count * cells) ** -0.5)
    devices = brick_count * group_count
    unit_rows = 16
    while devices * unit_rows * LANES < rows * cols or cols // 2 % unit_rows:
        unit_rows += 16
    unit = (unit_rows, LANES)
    peers = max(brick_count, group_count)
    vmem = pl.BlockSpec(memory_space=pltpu.VMEM)
    smem = pl.BlockSpec(memory_space=pltpu.SMEM)
    grad_fields, g1, g2 = pl.pallas_call(
        functools.partial(level_kernel, factor),
        out_shape=(
            jax.ShapeDtypeStruct((slots, channels, cells), BF),
            jax.ShapeDtypeStruct((cols, rows), F32),
            jax.ShapeDtypeStruct((cols, rows), F32),
        ),
        in_specs=[smem, smem] + [vmem] * 5,
        out_specs=(vmem, vmem, vmem),
        scratch_shapes=[
            pltpu.VMEM((slots + 1, channels, cells), BF),
            pltpu.VMEM((slots + 1, channels, cells + LANES), BF),
            pltpu.VMEM((slots + 1, rows, cells + LANES), BF),
            pltpu.VMEM((cols, cells + LANES), BF),
            pltpu.VMEM((slots, cols, cells), BF),
            pltpu.VMEM((slots, cols, cells), BF),
            pltpu.VMEM((slots, rows, cells), BF),
            pltpu.VMEM((slots, rows, cells), BF),
            pltpu.VMEM((2, slots, rows, cells), F32),
            pltpu.VMEM((slots, channels, cells), F32),
            pltpu.VMEM((slots, channels, cells), BF),
        ]
        + [pltpu.VMEM((3 * slots + 1, channels, LANES), BF)] * 4
        + [
            pltpu.VMEM((cols, 2 * LANES), F32),
            pltpu.VMEM((cols, 2 * LANES), F32),
            pltpu.VMEM((devices,) + unit, BF),
            pltpu.VMEM((brick_count,) + unit, BF),
            pltpu.VMEM((devices,) + unit, BF),
            pltpu.VMEM((group_count, brick_count) + unit, BF),
            pltpu.VMEM((brick_count,) + unit, BF),
            pltpu.VMEM((devices,) + unit, BF),
            pltpu.VMEM((brick_count,) + unit, BF),
            pltpu.VMEM((devices,) + unit, BF),
            pltpu.VMEM((group_count, brick_count) + unit, BF),
            pltpu.VMEM((brick_count,) + unit, BF),
            pltpu.SemaphoreType.DMA((4, 2)),
            pltpu.SemaphoreType.DMA((4, 2)),
            pltpu.SemaphoreType.DMA((8, peers)),
            pltpu.SemaphoreType.DMA((8, peers)),
        ],
        compiler_params=pltpu.CompilerParams(
            collective_id=0, has_side_effects=True, vmem_limit_bytes=50 * 1024 * 1024
        ),
    )(
        counts, adjacency[0], fields[0], cotangent[0],
        forward_w, backward_w(w2), backward_w(w1),
    )
    def weight_out(g):
        g = g.reshape(3, 3, channels, 3, channels)
        return jnp.transpose(g, (2, 4, 3, 0, 1)).reshape(channels, channels * 27)

    return (grad_fields[None], weight_out(g1), weight_out(g2))


def solution(mesh):
    return jax.shard_map(
        on_device,
        mesh=mesh,
        in_specs=(
            P("groups", "bricks", None, None),
            P("groups", "bricks", None, None),
            P(),
            P(),
            P("groups", "bricks"),
            P("groups", "bricks", None),
        ),
        out_specs=(P("groups", "bricks", None, None), P(), P()),
        check_vma=False,
    )
```
